32 devices in a mesh: pipe: 4 (over y, x), dp: 8 (over z, core).
Axes of the slice: x: 2, y: 2, z: 4, core: 2. Of those that a mesh axis runs over, the one named last changes fastest.
Arguments:
- grad_out: bfloat16 [4, 2, 2, 32, 3584], P('pipe', None, None, 'dp'), may hold values from -6 to 6
- hidden: bfloat16 [4, 2, 2, 32, 9216], P('pipe', None, None, None, 'dp'), may hold values from -5 to 5
- weights: bfloat16 [4, 9216, 3584], P('pipe', 'dp'), may hold values from -5 to 5
- counts: int32 [4, 2, 2, 8], P('pipe', None, None, 'dp'), may hold values from 1 to 4
Outputs:
- grad_hidden: bfloat16 [4, 2, 2, 32, 9216], P('pipe', None, None, None, 'dp')
- new_weights: bfloat16 [4, 9216, 3584], P('pipe', 'dp')
The draws below stay inside these ranges and needn't reach their ends.
All inputs are finite; a program needn't handle non-finite values.
Results may differ from the reference program's by a relative error of at most 0.0034.
Values may be sent and summed in bfloat16 or wider, within the bound.
A program may use at most 64 MiB of HBM per device.

```python
import jax
import jax.numpy as jnp
from jax import lax

D = 3584
H = 9216
M = 2
ROWS = 4
TOKROWS = 32
N_PIPE = 4
N_DP = 8


def with_ends(array, key, least, high):
    index_at = [jax.random.randint(jax.random.fold_in(key, axis), (), 0, length) for axis, length in enumerate(array.shape)]
    widest = array.shape.index(max(array.shape))
    neighbour = index_at[:widest] + [(index_at[widest] + 1) % array.shape[widest]] + index_at[widest + 1:]
    return array.at[tuple(index_at)].set(least).at[tuple(neighbour)].set(high)


def block_levels(rng, dims, pieces, smallest, high):
    def one(axis_at, blocks):
        draws = jax.random.uniform(jax.random.fold_in(jax.random.fold_in(rng, 6), axis_at), (blocks,), jnp.float32, smallest / len(pieces), high / len(pieces))
        return jnp.repeat(jnp.exp(draws), dims[axis_at] // blocks).reshape((-1,) + (1,) * (len(dims) - axis_at - 1))

    loudness = one(*pieces[0])
    for cut in pieces[1:]:
        loudness = loudness * one(*cut)
    return loudness


def bell_draw(key, extent, width, limit, pieces=(), held_as=jnp.bfloat16):
    drawn = width * jax.random.normal(key, extent, jnp.float32)
    if pieces:
        drawn = drawn * block_levels(key, extent, pieces, -0.22, 0.18)
    return jnp.clip(drawn, -limit, limit).astype(held_as)


def setup_inputs(seed: int = 0) -> dict:
    key_list = jax.random.split(jax.random.key(seed), 5)
    return {
        "grad_out": bell_draw(key_list[0], (N_PIPE, 2, M, TOKROWS, D), 1.0, 6.0, ((0, 4), (3, 8))),
        "hidden": bell_draw(key_list[1], (N_PIPE, 2, M, TOKROWS, H), 1.0, 5.0, ((0, 4), (4, 8))),
        "weights": bell_draw(key_list[2], (N_PIPE, H, D), 1.0, 5.0, ((0, 4), (1, 8))),
        "counts": with_ends(jax.random.randint(key_list[3], (N_PIPE, 2, M, N_DP), 1, ROWS + 1), jax.random.fold_in(key_list[3], 1), 1, ROWS).astype(jnp.int32),
    }


step_rate = 2.0


def reference(grad_out, hidden, weights, counts):
    scale_factor = D ** -0.5
    slot_index = jnp.arange(ROWS * N_DP, dtype=jnp.int32) % ROWS
    live_rows = jnp.repeat(counts, ROWS, axis=3) > slot_index
    masked = jnp.where(live_rows[..., None], grad_out, jnp.zeros_like(grad_out))
    section_rows = jnp.stack([masked[:, 0], masked[::-1, 1]], axis=1)
    section_acts = jnp.stack([hidden[:, 0], hidden[::-1, 1]], axis=1)

    def one_section(items):
        rows, acts, section_weight = items
        rows_f32 = rows.astype(jnp.float32)
        weight_f32 = section_weight.astype(jnp.float32)
        grad_rows = (jnp.einsum("rmtd,hd->rmth", rows_f32, weight_f32) * scale_factor).astype(jnp.bfloat16)
        partial_value = (jnp.einsum("rmth,rmtd->rhd", acts.astype(jnp.float32), rows_f32) * scale_factor).astype(jnp.bfloat16)
        gradient = partial_value[0].astype(jnp.float32) + partial_value[1].astype(jnp.float32)
        return grad_rows, (weight_f32 - step_rate * gradient).astype(jnp.bfloat16)

    section_grads, new_weights = lax.map(one_section, (section_rows, section_acts, weights))
    grad_hidden = jnp.stack([section_grads[:, 0], section_grads[::-1, 1]], axis=1)
    return grad_hidden, new_weights
```

```python
import functools

import jax
import jax.numpy as jnp
from jax import lax
from jax.experimental import pallas as pl
from jax.experimental.pallas import tpu as pltpu
from jax.sharding import PartitionSpec as P

step_rate = 2.0
MESH = pl.DeviceIdType.MESH
LEFT, RIGHT, SIBLING = 0, 1, 2


def when(condition, action):
    if condition is True:
        action()
    else:
        pl.when(condition)(action)


def gather_kernel(
    n_pipe, n_dp, scale_factor, chunk,
    counts_ref, grad_ref, hidden_ref, weights_ref,
    rows_ref, acts_ref, out_ref,
    staged, own_slot1, own_weight, own_hidden, mirror_hidden, ret,
    send_sem, recv_sem, pair_send, pair_recv, ret_send, ret_recv, load_sem,
):
    p = lax.axis_index("pipe")
    k = lax.axis_index("dp")
    z = k // 2
    n = n_dp // 2
    mirror = (n_pipe - 1 - p, k)
    sibling = k + 1 - 2 * (k % 2)
    has_left = z > 0
    has_right = z < n - 1
    micro, row_total, width = grad_ref.shape[2], grad_ref.shape[3], grad_ref.shape[4]
    half = width // 2
    block_rows = micro * row_total
    group_rows = hidden_ref.shape[3]
    share = hidden_ref.shape[4]

    load_hidden = pltpu.make_async_copy(hidden_ref.at[0], own_hidden, load_sem.at[0])
    load_weight = pltpu.make_async_copy(weights_ref.at[0], own_weight, load_sem.at[1])
    load_hidden.start()
    load_weight.start()

    barrier = pltpu.get_barrier_semaphore()
    pl.semaphore_signal(barrier, inc=1, device_id=mirror, device_id_type=MESH)
    pl.semaphore_signal(barrier, inc=1, device_id=(p, sibling), device_id_type=MESH)

    @pl.when(has_left)
    def _():
        pl.semaphore_signal(barrier, inc=1, device_id=(p, k - 2), device_id_type=MESH)

    @pl.when(has_right)
    def _():
        pl.semaphore_signal(barrier, inc=1, device_id=(p, k + 2), device_id_type=MESH)

    slot_index = lax.broadcasted_iota(jnp.int32, (row_total, width), 0)
    for r in (1, 0):
        for m in range(micro):
            live = slot_index < counts_ref[0, r, m, 0]
            rows = jnp.where(live, grad_ref[0, r, m].astype(jnp.float32), 0.0)
            for h in range(2):
                staged[r, pl.ds(h * block_rows + m * row_total, row_total), :] = rows[:, h * half:(h + 1) * half]
        packed = staged[r].astype(jnp.bfloat16)
        if r == 1:
            own_slot1[...] = packed
        else:
            rows_ref[0, k] = packed

    pl.semaphore_wait(barrier, 2 + has_left.astype(jnp.int32) + has_right.astype(jnp.int32))

    def hop(s, origin, way):
        target = {LEFT: k - 2, RIGHT: k + 2, SIBLING: sibling}[way]
        return pltpu.make_async_remote_copy(
            src_ref=rows_ref.at[s, origin],
            dst_ref=rows_ref.at[s, origin],
            send_sem=send_sem.at[s, origin, way],
            recv_sem=recv_sem.at[s, origin],
            device_id=(p, target),
            device_id_type=MESH,
        )

    def arrived(s, origin):
        hop(s, origin, SIBLING).wait_recv()

    mirror_rows = pltpu.make_async_remote_copy(
        src_ref=own_slot1, dst_ref=rows_ref.at[1, k],
        send_sem=pair_send.at[0], recv_sem=recv_sem.at[1, k],
        device_id=mirror, device_id_type=MESH,
    )
    mirror_acts = pltpu.make_async_remote_copy(
        src_ref=own_hidden.at[1], dst_ref=mirror_hidden,
        send_sem=pair_send.at[1], recv_sem=pair_recv.at[1],
        device_id=mirror, device_id_type=MESH,
    )

    sent = []

    def send(s, origin, way, condition):
        sent.append((s, origin, way, condition))
        when(condition, lambda: hop(s, origin, way).start())

    def send_own(s):
        send(s, k, LEFT, has_left)
        send(s, k, RIGHT, has_right)
        send(s, k, SIBLING, True)

    def relay(s, j):
        from_left = z >= j
        from_right = z + j < n
        left_origin = jnp.maximum(k - 2 * j, 0)
        right_origin = jnp.minimum(k + 2 * j, n_dp - 1)
        pl.when(from_left)(lambda: arrived(s, left_origin))
        send(s, left_origin, RIGHT, jnp.logical_and(from_left, has_right))
        send(s, left_origin, SIBLING, from_left)
        pl.when(from_right)(lambda: arrived(s, right_origin))
        send(s, right_origin, LEFT, jnp.logical_and(from_right, has_left))
        send(s, right_origin, SIBLING, from_right)

    mirror_rows.start()
    send_own(0)
    load_hidden.wait()
    mirror_acts.start()
    arrived(1, k)
    send_own(1)
    for j in range(1, n - 1):
        relay(0, j)
        relay(1, j)

    mirror_acts.wait_recv()
    tokens = micro * group_rows
    gathered = n_dp * 2 * block_rows
    at_row = lax.broadcasted_iota(jnp.int32, (gathered, tokens), 0)
    at_token = lax.broadcasted_iota(jnp.int32, (gathered, tokens), 1)
    rank, inside = at_row // (2 * block_rows), at_row % (2 * block_rows)
    which_half, inside = inside // block_rows, inside % block_rows
    wanted = (inside // row_total) * group_rows + rank * row_total + inside % row_total
    for h in range(2):
        place = jnp.where((wanted == at_token) & (which_half == h), 1.0, 0.0).astype(jnp.bfloat16)
        for s in range(2):
            acts = (own_hidden[0] if s == 0 else mirror_hidden[...]).reshape(tokens, share)
            acts_ref[h, :, pl.ds(s * gathered, gathered)] = lax.dot_general(
                acts, place, (((0,), (1,)), ((), ())), preferred_element_type=jnp.float32
            ).astype(jnp.bfloat16)

    if n > 1:
        relay(0, n - 1)
        relay(1, n - 1)
    load_weight.wait()

    out_token = lax.broadcasted_iota(jnp.int32, (tokens, tokens), 0)
    in_token = lax.broadcasted_iota(jnp.int32, (tokens, tokens), 1)
    out_m, out_t = out_token // group_rows, out_token % group_rows
    source = (out_t // row_total) * block_rows + out_m * row_total + out_t % row_total
    unplace = jnp.where(source == in_token, 1.0, 0.0).astype(jnp.bfloat16)

    def product(s, c):
        rows = rows_ref[s].reshape(gathered, half)
        parts = []
        for h in range(2):
            part = lax.dot_general(
                rows, own_weight[pl.ds(c * chunk, chunk), pl.ds(h * half, half)],
                (((1,), (1,)), ((), ())), preferred_element_type=jnp.float32,
            ).reshape(n_dp, 2, block_rows, chunk)
            parts.append(part[:, h])
        total = ((parts[0] + parts[1]) * scale_factor).astype(jnp.bfloat16).astype(jnp.float32)
        total = total.reshape(tokens, chunk).astype(jnp.bfloat16)
        return jnp.dot(unplace, total, preferred_element_type=jnp.float32).astype(
            jnp.bfloat16
        ).reshape(micro, group_rows, chunk)

    def give_back(c):
        columns = pl.ds(c * chunk, chunk)
        return pltpu.make_async_remote_copy(
            src_ref=ret.at[:, :, columns], dst_ref=out_ref.at[0, 1, :, :, columns],
            send_sem=ret_send.at[c], recv_sem=ret_recv.at[c],
            device_id=mirror, device_id_type=MESH,
        )

    for s in (1, 0):
        for j in range(n):
            for origin, there in ((sibling - 2 * j, z >= j), (sibling + 2 * j, z + j < n)):
                if j == 0 and origin is not None and there is not None:
                    pass
                safe = jnp.clip(origin, 0, n_dp - 1)
                if j == 0:
                    arrived(s, sibling)
                    break
                pl.when(there)(functools.partial(arrived, s, safe))
        for c in range(share // chunk):
            value = product(s, c)
            if s == 1:
                ret[:, :, pl.ds(c * chunk, chunk)] = value
                give_back(c).start()
            else:
                out_ref[0, 0, :, :, pl.ds(c * chunk, chunk)] = value

    mirror_rows.wait_send()
    mirror_acts.wait_send()
    for s, origin, way, condition in sent:
        when(condition, functools.partial(lambda *a: hop(*a).wait_send(), s, origin, way))
    for c in range(share // chunk):
        give_back(c).wait()


def update_kernel(factor, weights_ref, acts_ref, rows_ref, new_ref):
    half = rows_ref.shape[1]
    for h in range(2):
        columns = pl.ds(h * half, half)
        total = jnp.dot(acts_ref[h], rows_ref[...], preferred_element_type=jnp.float32)
        new_ref[0, :, columns] = (
            weights_ref[0, :, columns].astype(jnp.float32) - factor * total
        ).astype(jnp.bfloat16)


def shards(n_pipe, n_dp, grad_out, hidden, weights, counts):
    _, _, micro, row_total, width = grad_out.shape
    group_rows, share = hidden.shape[3], hidden.shape[4]
    block = 2 * micro * row_total
    half = width // 2
    gathered = n_dp * block
    scale_factor = float(width) ** (-0.5)
    chunk = 384 if share % 384 == 0 else share
    step = max(b for b in range(16, 193, 16) if share % b == 0)
    vmem = pl.BlockSpec(memory_space=pltpu.VMEM)
    hbm = pl.BlockSpec(memory_space=pl.ANY)
    rows, acts, grad_hidden = pl.pallas_call(
        functools.partial(gather_kernel, n_pipe, n_dp, scale_factor, chunk),
        out_shape=(
            jax.ShapeDtypeStruct((2, n_dp, block, half), jnp.bfloat16),
            jax.ShapeDtypeStruct((2, share, 2 * gathered), jnp.bfloat16),
            jax.ShapeDtypeStruct(hidden.shape, jnp.bfloat16),
        ),
        in_specs=[pl.BlockSpec(memory_space=pltpu.SMEM), vmem, hbm, hbm],
        out_specs=(vmem, vmem, vmem),
        scratch_shapes=[
            pltpu.VMEM((2, block, half), jnp.float32),
            pltpu.VMEM((block, half), jnp.bfloat16),
            pltpu.VMEM((share, width), jnp.bfloat16),
            pltpu.VMEM((2, micro, group_rows, share), jnp.bfloat16),
            pltpu.VMEM((micro, group_rows, share), jnp.bfloat16),
            pltpu.VMEM((micro, group_rows, share), jnp.bfloat16),
            pltpu.SemaphoreType.DMA((2, n_dp, 3)),
            pltpu.SemaphoreType.DMA((2, n_dp)),
            pltpu.SemaphoreType.DMA((2,)),
            pltpu.SemaphoreType.DMA((2,)),
            pltpu.SemaphoreType.DMA((share // chunk,)),
            pltpu.SemaphoreType.DMA((share // chunk,)),
            pltpu.SemaphoreType.DMA((2,)),
        ],
        compiler_params=pltpu.CompilerParams(
            collective_id=0, has_side_effects=True, vmem_limit_bytes=36 * 2**20
        ),
        name="gather",
    )(counts, grad_out, hidden, weights)
    new_weights = pl.pallas_call(
        functools.partial(update_kernel, step_rate * scale_factor),
        grid=(share // step,),
        out_shape=jax.ShapeDtypeStruct(weights.shape, jnp.bfloat16),
        in_specs=[
            pl.BlockSpec((1, step, width), lambda i: (0, i, 0)),
            pl.BlockSpec((2, step, 2 * gathered), lambda i: (0, i, 0)),
            pl.BlockSpec((2 * gathered, half), lambda i: (0, 0)),
        ],
        out_specs=pl.BlockSpec((1, step, width), lambda i: (0, i, 0)),
        compiler_params=pltpu.CompilerParams(vmem_limit_bytes=24 * 2**20),
        name="update",
    )(weights, acts, rows.reshape(2 * gathered, half))
    return grad_hidden, new_weights


def solution(mesh):
    return jax.shard_map(
        functools.partial(shards, mesh.shape["pipe"], mesh.shape["dp"]),
        mesh=mesh,
        in_specs=(
            P("pipe", None, None, "dp", None),
            P("pipe", None, None, None, "dp"),
            P("pipe", "dp", None),
            P("pipe", None, None, "dp"),
        ),
        out_specs=(P("pipe", None, None, None, "dp"), P("pipe", "dp", None)),
        check_vma=False,
    )
```

```python
import functools

import jax
import jax.numpy as jnp
from jax import lax
from jax.experimental import pallas as pl
from jax.experimental.pallas import tpu as pltpu
from jax.sharding import PartitionSpec as P

step_rate = 2.0
MESH = pl.DeviceIdType.MESH
LEFT, RIGHT, SIBLING = 0, 1, 2


def when(condition, action):
    if condition is True:
        action()
    else:
        pl.when(condition)(action)


def gather_kernel(
    n_pipe, n_dp, scale_factor, chunk,
    counts_ref, grad_ref, hidden_ref, weights_ref,
    rows_ref, acts_ref, weight_out, out_ref,
    own_grad, staged, own_slot1, landed, acts_in, ret,
    send_sem, recv_sem, pair_send, pair_recv, ret_send, ret_recv, load_sem,
):
    p = lax.axis_index("pipe")
    k = lax.axis_index("dp")
    z = k // 2
    n = n_dp // 2
    mirror = (n_pipe - 1 - p, k)
    sibling = k + 1 - 2 * (k % 2)
    has_left = z > 0
    has_right = z < n - 1
    micro, row_total, width = grad_ref.shape[2], grad_ref.shape[3], grad_ref.shape[4]
    half = width // 2
    block_rows = micro * row_total
    group_rows = hidden_ref.shape[3]
    share = hidden_ref.shape[4]
    tokens = 2 * micro * group_rows

    load_grad = pltpu.make_async_copy(grad_ref.at[0], own_grad, load_sem.at[0])
    load_acts = pltpu.make_async_copy(hidden_ref.at[0, 0], acts_in.at[0], load_sem.at[1])
    load_weight = pltpu.make_async_copy(weights_ref.at[0], weight_out, load_sem.at[2])
    load_grad.start()

    barrier = pltpu.get_barrier_semaphore()
    pl.semaphore_signal(barrier, inc=1, device_id=mirror, device_id_type=MESH)
    pl.semaphore_signal(barrier, inc=1, device_id=(p, sibling), device_id_type=MESH)

    @pl.when(has_left)
    def _():
        pl.semaphore_signal(barrier, inc=1, device_id=(p, k - 2), device_id_type=MESH)

    @pl.when(has_right)
    def _():
        pl.semaphore_signal(barrier, inc=1, device_id=(p, k + 2), device_id_type=MESH)

    load_acts.start()
    load_weight.start()
    load_grad.wait()
    slot_index = lax.broadcasted_iota(jnp.int32, (row_total, width), 0)
    for r in (1, 0):
        for m in range(micro):
            live = slot_index < counts_ref[r, m]
            rows = jnp.where(live, own_grad[r, m].astype(jnp.float32), 0.0)
            for h in range(2):
                staged[r, pl.ds(h * block_rows + m * row_total, row_total), :] = rows[:, h * half:(h + 1) * half]
        packed = staged[r].astype(jnp.bfloat16)
        if r == 1:
            own_slot1[...] = packed
        else:
            landed[0, k] = packed

    pl.semaphore_wait(barrier, 2 + has_left.astype(jnp.int32) + has_right.astype(jnp.int32))

    def hop(s, origin, way):
        target = {LEFT: k - 2, RIGHT: k + 2, SIBLING: sibling}[way]
        return pltpu.make_async_remote_copy(
            src_ref=landed.at[s, origin],
            dst_ref=landed.at[s, origin],
            send_sem=send_sem.at[s, origin, way],
            recv_sem=recv_sem.at[s, origin],
            device_id=(p, target),
            device_id_type=MESH,
        )

    def arrived(s, origin):
        hop(s, origin, SIBLING).wait_recv()

    mirror_rows = pltpu.make_async_remote_copy(
        src_ref=own_slot1, dst_ref=landed.at[1, k],
        send_sem=pair_send.at[0], recv_sem=recv_sem.at[1, k],
        device_id=mirror, device_id_type=MESH,
    )
    mirror_acts = pltpu.make_async_remote_copy(
        src_ref=hidden_ref.at[0, 1], dst_ref=acts_in.at[1],
        send_sem=pair_send.at[1], recv_sem=pair_recv.at[1],
        device_id=mirror, device_id_type=MESH,
    )

    sent = []

    def send(s, origin, way, condition):
        sent.append((s, origin, way, condition))
        when(condition, lambda: hop(s, origin, way).start())

    def send_own(s):
        send(s, k, LEFT, has_left)
        send(s, k, RIGHT, has_right)
        send(s, k, SIBLING, True)

    def relay(s, j):
        from_left = z >= j
        from_right = z + j < n
        left_origin = jnp.maximum(k - 2 * j, 0)
        right_origin = jnp.minimum(k + 2 * j, n_dp - 1)
        pl.when(from_left)(lambda: arrived(s, left_origin))
        send(s, left_origin, RIGHT, jnp.logical_and(from_left, has_right))
        send(s, left_origin, SIBLING, from_left)
        pl.when(from_right)(lambda: arrived(s, right_origin))
        send(s, right_origin, LEFT, jnp.logical_and(from_right, has_left))
        send(s, right_origin, SIBLING, from_right)

    mirror_rows.start()
    send_own(0)
    mirror_acts.start()
    arrived(1, k)
    send_own(1)
    for j in range(1, n - 1):
        relay(0, j)
        relay(1, j)

    at_token = lax.broadcasted_iota(jnp.int32, (tokens, tokens), 0)
    at_row = lax.broadcasted_iota(jnp.int32, (tokens, tokens), 1)
    slot, inside = at_token // (micro * group_rows), at_token % (micro * group_rows)
    of_micro, of_slot = inside // group_rows, inside % group_rows
    wanted = (
        slot * (micro * group_rows) + (of_slot // row_total) * block_rows
        + of_micro * row_total + of_slot % row_total
    )
    order = jnp.where(wanted == at_row, 1.0, 0.0).astype(jnp.bfloat16)

    load_acts.wait()
    mirror_acts.wait_recv()
    acts_ref[...] = lax.dot_general(
        acts_in[...].reshape(tokens, share), order,
        (((0,), (0,)), ((), ())), preferred_element_type=jnp.float32,
    ).astype(jnp.bfloat16)

    if n > 1:
        relay(0, n - 1)
        relay(1, n - 1)

    for s in range(2):
        arrived(s, sibling)
        for j in range(1, n):
            pl.when(z >= j)(functools.partial(arrived, s, jnp.maximum(sibling - 2 * j, 0)))
            pl.when(z + j < n)(functools.partial(arrived, s, jnp.minimum(sibling + 2 * j, n_dp - 1)))
        for h in range(2):
            blocks = [
                landed[s, rank].astype(jnp.float32)[h * block_rows:(h + 1) * block_rows]
                for rank in range(n_dp)
            ]
            rows_ref[pl.ds(s * (tokens // 2), tokens // 2), pl.ds(h * half, half)] = jnp.concatenate(
                blocks, axis=0
            ).astype(jnp.bfloat16)
    load_weight.wait()

    def give_back(c):
        columns = pl.ds(c * chunk, chunk)
        return pltpu.make_async_remote_copy(
            src_ref=ret.at[:, :, columns], dst_ref=out_ref.at[0, 1, :, :, columns],
            send_sem=ret_send.at[c], recv_sem=ret_recv.at[c],
            device_id=mirror, device_id_type=MESH,
        )

    for c in range(share // chunk):
        columns = pl.ds(c * chunk, chunk)
        product = lax.dot_general(
            weight_out[columns, :], rows_ref[...],
            (((1,), (1,)), ((), ())), preferred_element_type=jnp.float32,
        )
        rounded = (product * scale_factor).astype(jnp.bfloat16)
        value = lax.dot_general(
            order, rounded, (((1,), (1,)), ((), ())), preferred_element_type=jnp.float32
        ).astype(jnp.bfloat16).reshape(2, micro, group_rows, chunk)
        ret[:, :, columns] = value[1]
        give_back(c).start()
        out_ref[0, 0, :, :, columns] = value[0]

    mirror_rows.wait_send()
    mirror_acts.wait_send()
    for s, origin, way, condition in sent:
        when(condition, functools.partial(lambda *a: hop(*a).wait_send(), s, origin, way))
    for c in range(share // chunk):
        give_back(c).wait()


def update_kernel(
    factor, step, weight_ref, acts_ref, rows_ref, back_ref, new_ref, out_ref, slots, sems, out_sem
):
    put_back = pltpu.make_async_copy(back_ref, out_ref, out_sem)
    put_back.start()
    depth = slots.shape[0]
    steps = weight_ref.shape[1] // step

    def put(i):
        return pltpu.make_async_copy(
            slots.at[i % depth], new_ref.at[0, :, pl.ds(i * step, step)], sems.at[i % depth]
        )

    for i in range(steps):
        columns = pl.ds(i * step, step)
        if i >= depth:
            put(i - depth).wait()
        total = jnp.dot(acts_ref[...], rows_ref[:, columns], preferred_element_type=jnp.float32)
        slots[i % depth] = (
            weight_ref[:, columns].astype(jnp.float32) - factor * total
        ).astype(jnp.bfloat16)
        put(i).start()
    for i in range(max(0, steps - depth), steps):
        put(i).wait()
    put_back.wait()


def shards(n_pipe, n_dp, grad_out, hidden, weights, counts):
    _, _, micro, row_total, width = grad_out.shape
    group_rows, share = hidden.shape[3], hidden.shape[4]
    block = 2 * micro * row_total
    half = width // 2
    tokens = 2 * micro * group_rows
    scale_factor = float(width) ** (-0.5)
    chunk = 384 if share % 384 == 0 else share
    step = 256 if width % 256 == 0 else 128
    vmem = pl.BlockSpec(memory_space=pltpu.VMEM)
    hbm = pl.BlockSpec(memory_space=pltpu.HBM)
    rows, acts, weight, back = pl.pallas_call(
        functools.partial(gather_kernel, n_pipe, n_dp, scale_factor, chunk),
        out_shape=(
            jax.ShapeDtypeStruct((tokens, width), jnp.bfloat16),
            jax.ShapeDtypeStruct((share, tokens), jnp.bfloat16),
            jax.ShapeDtypeStruct((share, width), jnp.bfloat16),
            jax.ShapeDtypeStruct(hidden.shape, jnp.bfloat16),
        ),
        in_specs=[pl.BlockSpec(memory_space=pltpu.SMEM), hbm, hbm, hbm],
        out_specs=(vmem, vmem, vmem, vmem),
        scratch_shapes=[
            pltpu.VMEM((2, micro, row_total, width), jnp.bfloat16),
            pltpu.VMEM((2, block, half), jnp.float32),
            pltpu.VMEM((block, half), jnp.bfloat16),
            pltpu.VMEM((2, n_dp, block, half), jnp.bfloat16),
            pltpu.VMEM((2, micro, group_rows, share), jnp.bfloat16),
            pltpu.VMEM((micro, group_rows, share), jnp.bfloat16),
            pltpu.SemaphoreType.DMA((2, n_dp, 3)),
            pltpu.SemaphoreType.DMA((2, n_dp)),
            pltpu.SemaphoreType.DMA((2,)),
            pltpu.SemaphoreType.DMA((2,)),
            pltpu.SemaphoreType.DMA((share // chunk,)),
            pltpu.SemaphoreType.DMA((share // chunk,)),
            pltpu.SemaphoreType.DMA((3,)),
        ],
        compiler_params=pltpu.CompilerParams(
            collective_id=0, has_side_effects=True, vmem_limit_bytes=42 * 2**20
        ),
        name="gather",
    )(counts.reshape(2, micro), grad_out, hidden, weights)
    new_weights, grad_hidden = pl.pallas_call(
        functools.partial(update_kernel, step_rate * scale_factor, step),
        out_shape=(
            jax.ShapeDtypeStruct(weights.shape, jnp.bfloat16),
            jax.ShapeDtypeStruct(hidden.shape, jnp.bfloat16),
        ),
        in_specs=[vmem, vmem, vmem, vmem],
        out_specs=(hbm, hbm),
        scratch_shapes=[
            pltpu.VMEM((4, share, step), jnp.bfloat16),
            pltpu.SemaphoreType.DMA((4,)),
            pltpu.SemaphoreType.DMA,
        ],
        compiler_params=pltpu.CompilerParams(vmem_limit_bytes=24 * 2**20),
        name="update",
    )(weight, acts, rows, back)
    return grad_hidden, new_weights


def solution(mesh):
    return jax.shard_map(
        functools.partial(shards, mesh.shape["pipe"], mesh.shape["dp"]),
        mesh=mesh,
        in_specs=(
            P("pipe", None, None, "dp", None),
            P("pipe", None, None, None, "dp"),
            P("pipe", "dp", None),
            P("pipe", None, None, "dp"),
        ),
        out_specs=(P("pipe", None, None, None, "dp"), P("pipe", "dp", None)),
        check_vma=False,
    )
```

```python
import functools

import jax
import jax.numpy as jnp
from jax import lax
from jax.experimental import pallas as pl
from jax.experimental.pallas import tpu as pltpu
from jax.sharding import PartitionSpec as P

step_rate = 2.0
MESH = pl.DeviceIdType.MESH
LEFT, RIGHT, SIBLING = 0, 1, 2


def when(condition, action):
    if condition is True:
        action()
    else:
        pl.when(condition)(action)


def update_rows(factor, weight_ref, acts_ref, rows_ref, target_ref, first, count, target_first):
    high = 192 if count % 192 == 0 else count
    wide = 256 if weight_ref.shape[1] % 256 == 0 else 128
    for r in range(0, count, high):
        for c in range(0, weight_ref.shape[1], wide):
            columns = pl.ds(c, wide)
            total = jnp.dot(
                acts_ref[pl.ds(first + r, high), :], rows_ref[:, columns], preferred_element_type=jnp.float32
            )
            target_ref[pl.ds(target_first + r, high), columns] = (
                weight_ref[pl.ds(first + r, high), columns].astype(jnp.float32) - factor * total
            ).astype(jnp.bfloat16)


def gather_kernel(
    n_pipe, n_dp, scale_factor, chunk, early,
    counts_ref, grad_ref, hidden_ref, weights_ref,
    rows_ref, acts_ref, weight_out, out_ref,
    own_grad, staged, own_slot1, landed, acts_in, ret,
    send_sem, recv_sem, pair_send, pair_recv, ret_send, ret_recv, load_sem,
):
    p = lax.axis_index("pipe")
    k = lax.axis_index("dp")
    z = k // 2
    n = n_dp // 2
    mirror = (n_pipe - 1 - p, k)
    sibling = k + 1 - 2 * (k % 2)
    has_left = z > 0
    has_right = z < n - 1
    micro, row_total, width = grad_ref.shape[2], grad_ref.shape[3], grad_ref.shape[4]
    half = width // 2
    block_rows = micro * row_total
    group_rows = hidden_ref.shape[3]
    share = hidden_ref.shape[4]
    tokens = 2 * micro * group_rows

    load_grad = pltpu.make_async_copy(grad_ref.at[0], own_grad, load_sem.at[0])
    load_acts = pltpu.make_async_copy(hidden_ref.at[0, 0], acts_in.at[0], load_sem.at[1])
    load_weight = pltpu.make_async_copy(weights_ref.at[0], weight_out, load_sem.at[2])
    load_grad.start()

    barrier = pltpu.get_barrier_semaphore()
    pl.semaphore_signal(barrier, inc=1, device_id=mirror, device_id_type=MESH)
    pl.semaphore_signal(barrier, inc=1, device_id=(p, sibling), device_id_type=MESH)

    @pl.when(has_left)
    def _():
        pl.semaphore_signal(barrier, inc=1, device_id=(p, k - 2), device_id_type=MESH)

    @pl.when(has_right)
    def _():
        pl.semaphore_signal(barrier, inc=1, device_id=(p, k + 2), device_id_type=MESH)

    load_acts.start()
    load_weight.start()
    load_grad.wait()
    slot_index = lax.broadcasted_iota(jnp.int32, (row_total, width), 0)
    for r in (1, 0):
        for m in range(micro):
            live = slot_index < counts_ref[r, m]
            rows = jnp.where(live, own_grad[r, m].astype(jnp.float32), 0.0)
            for h in range(2):
                staged[r, pl.ds(h * block_rows + m * row_total, row_total), :] = rows[:, h * half:(h + 1) * half]
        packed = staged[r].astype(jnp.bfloat16)
        if r == 1:
            own_slot1[...] = packed
        else:
            landed[0, k] = packed

    pl.semaphore_wait(barrier, 2 + has_left.astype(jnp.int32) + has_right.astype(jnp.int32))

    def hop(s, origin, way):
        target = {LEFT: k - 2, RIGHT: k + 2, SIBLING: sibling}[way]
        return pltpu.make_async_remote_copy(
            src_ref=landed.at[s, origin],
            dst_ref=landed.at[s, origin],
            send_sem=send_sem.at[s, origin, way],
            recv_sem=recv_sem.at[s, origin],
            device_id=(p, target),
            device_id_type=MESH,
        )

    def arrived(s, origin):
        hop(s, origin, SIBLING).wait_recv()

    mirror_rows = pltpu.make_async_remote_copy(
        src_ref=own_slot1, dst_ref=landed.at[1, k],
        send_sem=pair_send.at[0], recv_sem=recv_sem.at[1, k],
        device_id=mirror, device_id_type=MESH,
    )
    mirror_acts = pltpu.make_async_remote_copy(
        src_ref=hidden_ref.at[0, 1], dst_ref=acts_in.at[1],
        send_sem=pair_send.at[1], recv_sem=pair_recv.at[1],
        device_id=mirror, device_id_type=MESH,
    )

    sent = []

    def send(s, origin, way, condition):
        sent.append((s, origin, way, condition))
        when(condition, lambda: hop(s, origin, way).start())

    def send_own(s):
        send(s, k, LEFT, has_left)
        send(s, k, RIGHT, has_right)
        send(s, k, SIBLING, True)

    def relay(s, j):
        from_left = z >= j
        from_right = z + j < n
        left_origin = jnp.maximum(k - 2 * j, 0)
        right_origin = jnp.minimum(k + 2 * j, n_dp - 1)
        pl.when(from_left)(lambda: arrived(s, left_origin))
        send(s, left_origin, RIGHT, jnp.logical_and(from_left, has_right))
        send(s, left_origin, SIBLING, from_left)
        pl.when(from_right)(lambda: arrived(s, right_origin))
        send(s, right_origin, LEFT, jnp.logical_and(from_right, has_left))
        send(s, right_origin, SIBLING, from_right)

    mirror_rows.start()
    send_own(0)
    mirror_acts.start()
    arrived(1, k)
    send_own(1)
    for j in range(1, n - 1):
        relay(0, j)
        relay(1, j)

    at_token = lax.broadcasted_iota(jnp.int32, (tokens, tokens), 0)
    at_row = lax.broadcasted_iota(jnp.int32, (tokens, tokens), 1)
    slot, inside = at_token // (micro * group_rows), at_token % (micro * group_rows)
    of_micro, of_slot = inside // group_rows, inside % group_rows
    wanted = (
        slot * (micro * group_rows) + (of_slot // row_total) * block_rows
        + of_micro * row_total + of_slot % row_total
    )
    order = jnp.where(wanted == at_row, 1.0, 0.0).astype(jnp.bfloat16)

    load_acts.wait()
    mirror_acts.wait_recv()
    acts_ref[...] = lax.dot_general(
        acts_in[...].reshape(tokens, share), order,
        (((0,), (0,)), ((), ())), preferred_element_type=jnp.float32,
    ).astype(jnp.bfloat16)

    if n > 1:
        relay(0, n - 1)
        relay(1, n - 1)

    for s in range(2):
        arrived(s, sibling)
        for j in range(1, n):
            pl.when(z >= j)(functools.partial(arrived, s, jnp.maximum(sibling - 2 * j, 0)))
            pl.when(z + j < n)(functools.partial(arrived, s, jnp.minimum(sibling + 2 * j, n_dp - 1)))
        for h in range(2):
            blocks = [
                landed[s, rank].astype(jnp.float32)[h * block_rows:(h + 1) * block_rows]
                for rank in range(n_dp)
            ]
            rows_ref[pl.ds(s * (tokens // 2), tokens // 2), pl.ds(h * half, half)] = jnp.concatenate(
                blocks, axis=0
            ).astype(jnp.bfloat16)
    load_weight.wait()

    def give_back(c):
        columns = pl.ds(c * chunk, chunk)
        return pltpu.make_async_remote_copy(
            src_ref=ret.at[:, :, columns], dst_ref=out_ref.at[0, 1, :, :, columns],
            send_sem=ret_send.at[c], recv_sem=ret_recv.at[c],
            device_id=mirror, device_id_type=MESH,
        )

    for c in range(share // chunk):
        columns = pl.ds(c * chunk, chunk)
        product = lax.dot_general(
            weight_out[columns, :], rows_ref[...],
            (((1,), (1,)), ((), ())), preferred_element_type=jnp.float32,
        )
        rounded = (product * scale_factor).astype(jnp.bfloat16)
        value = lax.dot_general(
            order, rounded, (((1,), (1,)), ((), ())), preferred_element_type=jnp.float32
        ).astype(jnp.bfloat16).reshape(2, micro, group_rows, chunk)
        ret[:, :, columns] = value[1]
        give_back(c).start()
        out_ref[0, 0, :, :, columns] = value[0]

    update_rows(step_rate * scale_factor, weight_out, acts_ref, rows_ref, weight_out, 0, early, 0)

    mirror_rows.wait_send()
    mirror_acts.wait_send()
    for s, origin, way, condition in sent:
        when(condition, functools.partial(lambda *a: hop(*a).wait_send(), s, origin, way))
    for c in range(share // chunk):
        give_back(c).wait()


def update_kernel(
    factor, early, step, weight_ref, acts_ref, rows_ref, back_ref, new_ref, out_ref, late, sems, out_sem
):
    put_back = pltpu.make_async_copy(back_ref, out_ref, out_sem)
    share = weight_ref.shape[0]

    def put(i):
        first = i * step
        source = weight_ref.at[pl.ds(first, step)] if first < early else late.at[pl.ds(first - early, step)]
        return pltpu.make_async_copy(source, new_ref.at[0, pl.ds(first, step)], sems.at[i])

    for i in range(early // step):
        put(i).start()
    put_back.start()
    for i in range(early // step, share // step):
        update_rows(factor, weight_ref, acts_ref, rows_ref, late, i * step, step, i * step - early)
        put(i).start()
    for i in range(share // step):
        put(i).wait()
    put_back.wait()


def shards(n_pipe, n_dp, grad_out, hidden, weights, counts):
    _, _, micro, row_total, width = grad_out.shape
    group_rows, share = hidden.shape[3], hidden.shape[4]
    block = 2 * micro * row_total
    half = width // 2
    tokens = 2 * micro * group_rows
    scale_factor = float(width) ** (-0.5)
    chunk = 384 if share % 384 == 0 else share
    early = 2 * (share // chunk) // 3 * chunk
    step = 192 if chunk % 192 == 0 else chunk
    vmem = pl.BlockSpec(memory_space=pltpu.VMEM)
    hbm = pl.BlockSpec(memory_space=pltpu.HBM)
    rows, acts, weight, back = pl.pallas_call(
        functools.partial(gather_kernel, n_pipe, n_dp, scale_factor, chunk, early),
        out_shape=(
            jax.ShapeDtypeStruct((tokens, width), jnp.bfloat16),
            jax.ShapeDtypeStruct((share, tokens), jnp.bfloat16),
            jax.ShapeDtypeStruct((share, width), jnp.bfloat16),
            jax.ShapeDtypeStruct(hidden.shape, jnp.bfloat16),
        ),
        in_specs=[pl.BlockSpec(memory_space=pltpu.SMEM), hbm, hbm, hbm],
        out_specs=(vmem, vmem, vmem, vmem),
        scratch_shapes=[
            pltpu.VMEM((2, micro, row_total, width), jnp.bfloat16),
            pltpu.VMEM((2, block, half), jnp.float32),
            pltpu.VMEM((block, half), jnp.bfloat16),
            pltpu.VMEM((2, n_dp, block, half), jnp.bfloat16),
            pltpu.VMEM((2, micro, group_rows, share), jnp.bfloat16),
            pltpu.VMEM((micro, group_rows, share), jnp.bfloat16),
            pltpu.SemaphoreType.DMA((2, n_dp, 3)),
            pltpu.SemaphoreType.DMA((2, n_dp)),
            pltpu.SemaphoreType.DMA((2,)),
            pltpu.SemaphoreType.DMA((2,)),
            pltpu.SemaphoreType.DMA((share // chunk,)),
            pltpu.SemaphoreType.DMA((share // chunk,)),
            pltpu.SemaphoreType.DMA((3,)),
        ],
        compiler_params=pltpu.CompilerParams(
            collective_id=0, has_side_effects=True, vmem_limit_bytes=42 * 2**20
        ),
        name="gather",
    )(counts.reshape(2, micro), grad_out, hidden, weights)
    new_weights, grad_hidden = pl.pallas_call(
        functools.partial(update_kernel, step_rate * scale_factor, early, step),
        out_shape=(
            jax.ShapeDtypeStruct(weights.shape, jnp.bfloat16),
            jax.ShapeDtypeStruct(hidden.shape, jnp.bfloat16),
        ),
        in_specs=[vmem, vmem, vmem, vmem],
        out_specs=(hbm, hbm),
        scratch_shapes=[
            pltpu.VMEM((share - early, width), jnp.bfloat16),
            pltpu.SemaphoreType.DMA((share // step,)),
            pltpu.SemaphoreType.DMA,
        ],
        compiler_params=pltpu.CompilerParams(vmem_limit_bytes=24 * 2**20),
        name="update",
    )(weight, acts, rows, back)
    return grad_hidden, new_weights


def solution(mesh):
    return jax.shard_map(
        functools.partial(shards, mesh.shape["pipe"], mesh.shape["dp"]),
        mesh=mesh,
        in_specs=(
            P("pipe", None, None, "dp", None),
            P("pipe", None, None, None, "dp"),
            P("pipe", "dp", None),
            P("pipe", None, None, "dp"),
        ),
        out_specs=(P("pipe", None, None, None, "dp"), P("pipe", "dp", None)),
        check_vma=False,
    )
```

```python
import functools

import jax
import jax.numpy as jnp
from jax import lax
from jax.experimental import pallas as pl
from jax.experimental.pallas import tpu as pltpu
from jax.sharding import PartitionSpec as P

step_rate = 2.0
MESH = pl.DeviceIdType.MESH
LEFT, RIGHT, SIBLING = 0, 1, 2


def when(condition, action):
    if condition is True:
        action()
    else:
        pl.when(condition)(action)


def update_rows(factor, weight_ref, acts_ref, rows_ref, target_ref, first, count, target_first):
    high = 192 if count % 192 == 0 else count
    wide = 256 if weight_ref.shape[1] % 256 == 0 else 128
    for r in range(0, count, high):
        for c in range(0, weight_ref.shape[1], wide):
            columns = pl.ds(c, wide)
            total = jnp.dot(
                acts_ref[pl.ds(first + r, high), :], rows_ref[:, columns], preferred_element_type=jnp.float32
            )
            target_ref[pl.ds(target_first + r, high), columns] = (
                weight_ref[pl.ds(first + r, high), columns].astype(jnp.float32) - factor * total
            ).astype(jnp.bfloat16)


def gather_kernel(
    n_pipe, n_dp, scale_factor, chunk, early,
    counts_ref, grad_ref, hidden_ref, weights_ref,
    rows_ref, acts_ref, weight_out, out_ref,
    own_grad, staged, own_slot1, landed, acts_in, ret,
    send_sem, recv_sem, pair_send, pair_recv, ret_send, ret_recv, load_sem,
):
    p = lax.axis_index("pipe")
    k = lax.axis_index("dp")
    z = k // 2
    n = n_dp // 2
    mirror = (n_pipe - 1 - p, k)
    sibling = k + 1 - 2 * (k % 2)
    has_left = z > 0
    has_right = z < n - 1
    micro, row_total, width = grad_ref.shape[2], grad_ref.shape[3], grad_ref.shape[4]
    half = width // 2
    block_rows = micro * row_total
    group_rows = hidden_ref.shape[3]
    share = hidden_ref.shape[4]
    tokens = 2 * micro * group_rows

    load_grad = pltpu.make_async_copy(grad_ref.at[0], own_grad, load_sem.at[0])
    load_acts = pltpu.make_async_copy(hidden_ref.at[0, 0], acts_in.at[0], load_sem.at[1])
    load_weight = pltpu.make_async_copy(weights_ref.at[0], weight_out, load_sem.at[2])
    load_grad.start()

    barrier = pltpu.get_barrier_semaphore()
    pl.semaphore_signal(barrier, inc=1, device_id=mirror, device_id_type=MESH)
    pl.semaphore_signal(barrier, inc=1, device_id=(p, sibling), device_id_type=MESH)

    @pl.when(has_left)
    def _():
        pl.semaphore_signal(barrier, inc=1, device_id=(p, k - 2), device_id_type=MESH)

    @pl.when(has_right)
    def _():
        pl.semaphore_signal(barrier, inc=1, device_id=(p, k + 2), device_id_type=MESH)

    load_acts.start()
    load_weight.start()
    load_grad.wait()
    slot_index = lax.broadcasted_iota(jnp.int32, (row_total, width), 0)
    for r in (1, 0):
        for m in range(micro):
            live = slot_index < counts_ref[r, m]
            rows = jnp.where(live, own_grad[r, m].astype(jnp.float32), 0.0)
            for h in range(2):
                staged[r, pl.ds(h * block_rows + m * row_total, row_total), :] = rows[:, h * half:(h + 1) * half]
        packed = staged[r].astype(jnp.bfloat16)
        if r == 1:
            own_slot1[...] = packed
        else:
            landed[0, k] = packed

    pl.semaphore_wait(barrier, 2 + has_left.astype(jnp.int32) + has_right.astype(jnp.int32))

    def hop(s, origin, way):
        target = {LEFT: k - 2, RIGHT: k + 2, SIBLING: sibling}[way]
        return pltpu.make_async_remote_copy(
            src_ref=landed.at[s, origin],
            dst_ref=landed.at[s, origin],
            send_sem=send_sem.at[s, origin, way],
            recv_sem=recv_sem.at[s, origin],
            device_id=(p, target),
            device_id_type=MESH,
        )

    def arrived(s, origin):
        hop(s, origin, SIBLING).wait_recv()

    mirror_rows = pltpu.make_async_remote_copy(
        src_ref=own_slot1, dst_ref=landed.at[1, k],
        send_sem=pair_send.at[0], recv_sem=recv_sem.at[1, k],
        device_id=mirror, device_id_type=MESH,
    )
    mirror_acts = pltpu.make_async_remote_copy(
        src_ref=hidden_ref.at[0, 1], dst_ref=acts_in.at[1],
        send_sem=pair_send.at[1], recv_sem=pair_recv.at[1],
        device_id=mirror, device_id_type=MESH,
    )

    sent = []

    def send(s, origin, way, condition):
        sent.append((s, origin, way, condition))
        when(condition, lambda: hop(s, origin, way).start())

    def send_own(s):
        send(s, k, LEFT, has_left)
        send(s, k, RIGHT, has_right)
        send(s, k, SIBLING, True)

    def relay(s, j):
        from_left = z >= j
        from_right = z + j < n
        left_origin = jnp.maximum(k - 2 * j, 0)
        right_origin = jnp.minimum(k + 2 * j, n_dp - 1)
        pl.when(from_left)(lambda: arrived(s, left_origin))
        send(s, left_origin, RIGHT, jnp.logical_and(from_left, has_right))
        send(s, left_origin, SIBLING, from_left)
        pl.when(from_right)(lambda: arrived(s, right_origin))
        send(s, right_origin, LEFT, jnp.logical_and(from_right, has_left))
        send(s, right_origin, SIBLING, from_right)

    def drain():
        for s, origin, way, condition in sent:
            when(condition, functools.partial(lambda *a: hop(*a).wait_send(), s, origin, way))
        sent.clear()

    mirror_rows.start()
    send_own(0)
    arrived(1, k)
    send_own(1)
    mirror_acts.start()
    for j in range(1, n - 1):
        drain()
        relay(0, j)
        relay(1, j)

    at_token = lax.broadcasted_iota(jnp.int32, (tokens, tokens), 0)
    at_row = lax.broadcasted_iota(jnp.int32, (tokens, tokens), 1)
    slot, inside = at_token // (micro * group_rows), at_token % (micro * group_rows)
    of_micro, of_slot = inside // group_rows, inside % group_rows
    wanted = (
        slot * (micro * group_rows) + (of_slot // row_total) * block_rows
        + of_micro * row_total + of_slot % row_total
    )
    order = jnp.where(wanted == at_row, 1.0, 0.0).astype(jnp.bfloat16)

    load_acts.wait()
    mirror_acts.wait_recv()
    acts_ref[...] = lax.dot_general(
        acts_in[...].reshape(tokens, share), order,
        (((0,), (0,)), ((), ())), preferred_element_type=jnp.float32,
    ).astype(jnp.bfloat16)

    if n > 1:
        relay(1, n - 1)
        relay(0, n - 1)

    for s in range(2):
        arrived(s, sibling)
        for j in range(1, n):
            pl.when(z >= j)(functools.partial(arrived, s, jnp.maximum(sibling - 2 * j, 0)))
            pl.when(z + j < n)(functools.partial(arrived, s, jnp.minimum(sibling + 2 * j, n_dp - 1)))
        for h in range(2):
            blocks = [
                landed[s, rank].astype(jnp.float32)[h * block_rows:(h + 1) * block_rows]
                for rank in range(n_dp)
            ]
            rows_ref[pl.ds(s * (tokens // 2), tokens // 2), pl.ds(h * half, half)] = jnp.concatenate(
                blocks, axis=0
            ).astype(jnp.bfloat16)
    load_weight.wait()

    def give_back(c):
        columns = pl.ds(c * chunk, chunk)
        return pltpu.make_async_remote_copy(
            src_ref=ret.at[:, :, columns], dst_ref=out_ref.at[0, 1, :, :, columns],
            send_sem=ret_send.at[c], recv_sem=ret_recv.at[c],
            device_id=mirror, device_id_type=MESH,
        )

    for c in range(share // chunk):
        columns = pl.ds(c * chunk, chunk)
        product = lax.dot_general(
            weight_out[columns, :], rows_ref[...],
            (((1,), (1,)), ((), ())), preferred_element_type=jnp.float32,
        )
        rounded = (product * scale_factor).astype(jnp.bfloat16)
        value = lax.dot_general(
            order, rounded, (((1,), (1,)), ((), ())), preferred_element_type=jnp.float32
        ).astype(jnp.bfloat16).reshape(2, micro, group_rows, chunk)
        ret[:, :, columns] = value[1]
        give_back(c).start()
        out_ref[0, 0, :, :, columns] = value[0]

    update_rows(step_rate * scale_factor, weight_out, acts_ref, rows_ref, weight_out, 0, early, 0)

    mirror_rows.wait_send()
    mirror_acts.wait_send()
    drain()
    for c in range(share // chunk):
        give_back(c).wait()


def update_kernel(
    factor, early, step, weight_ref, acts_ref, rows_ref, back_ref, new_ref, out_ref, late, sems, out_sem
):
    put_back = pltpu.make_async_copy(back_ref, out_ref, out_sem)
    share = weight_ref.shape[0]

    def put(i):
        first = i * step
        source = weight_ref.at[pl.ds(first, step)] if first < early else late.at[pl.ds(first - early, step)]
        return pltpu.make_async_copy(source, new_ref.at[0, pl.ds(first, step)], sems.at[i])

    for i in range(early // step):
        put(i).start()
    put_back.start()
    for i in range(early // step, share // step):
        update_rows(factor, weight_ref, acts_ref, rows_ref, late, i * step, step, i * step - early)
        put(i).start()
    for i in range(share // step):
        put(i).wait()
    put_back.wait()


def shards(n_pipe, n_dp, grad_out, hidden, weights, counts):
    _, _, micro, row_total, width = grad_out.shape
    group_rows, share = hidden.shape[3], hidden.shape[4]
    block = 2 * micro * row_total
    half = width // 2
    tokens = 2 * micro * group_rows
    scale_factor = float(width) ** (-0.5)
    chunk = 384 if share % 384 == 0 else share
    early = 2 * (share // chunk) // 3 * chunk
    step = 192 if chunk % 192 == 0 else chunk
    vmem = pl.BlockSpec(memory_space=pltpu.VMEM)
    hbm = pl.BlockSpec(memory_space=pltpu.HBM)
    rows, acts, weight, back = pl.pallas_call(
        functools.partial(gather_kernel, n_pipe, n_dp, scale_factor, chunk, early),
        out_shape=(
            jax.ShapeDtypeStruct((tokens, width), jnp.bfloat16),
            jax.ShapeDtypeStruct((share, tokens), jnp.bfloat16),
            jax.ShapeDtypeStruct((share, width), jnp.bfloat16),
            jax.ShapeDtypeStruct(hidden.shape, jnp.bfloat16),
        ),
        in_specs=[pl.BlockSpec(memory_space=pltpu.SMEM), hbm, hbm, hbm],
        out_specs=(vmem, vmem, vmem, vmem),
        scratch_shapes=[
            pltpu.VMEM((2, micro, row_total, width), jnp.bfloat16),
            pltpu.VMEM((2, block, half), jnp.float32),
            pltpu.VMEM((block, half), jnp.bfloat16),
            pltpu.VMEM((2, n_dp, block, half), jnp.bfloat16),
            pltpu.VMEM((2, micro, group_rows, share), jnp.bfloat16),
            pltpu.VMEM((micro, group_rows, share), jnp.bfloat16),
            pltpu.SemaphoreType.DMA((2, n_dp, 3)),
            pltpu.SemaphoreType.DMA((2, n_dp)),
            pltpu.SemaphoreType.DMA((2,)),
            pltpu.SemaphoreType.DMA((2,)),
            pltpu.SemaphoreType.DMA((share // chunk,)),
            pltpu.SemaphoreType.DMA((share // chunk,)),
            pltpu.SemaphoreType.DMA((3,)),
        ],
        compiler_params=pltpu.CompilerParams(
            collective_id=0, has_side_effects=True, vmem_limit_bytes=42 * 2**20
        ),
        name="gather",
    )(*[pltpu.with_memory_space_constraint(x, pltpu.HBM) for x in (counts.reshape(2, micro), grad_out, hidden, weights)])
    new_weights, grad_hidden = pl.pallas_call(
        functools.partial(update_kernel, step_rate * scale_factor, early, step),
        out_shape=(
            jax.ShapeDtypeStruct(weights.shape, jnp.bfloat16),
            jax.ShapeDtypeStruct(hidden.shape, jnp.bfloat16),
        ),
        in_specs=[vmem, vmem, vmem, vmem],
        out_specs=(hbm, hbm),
        scratch_shapes=[
            pltpu.VMEM((share - early, width), jnp.bfloat16),
            pltpu.SemaphoreType.DMA((share // step,)),
            pltpu.SemaphoreType.DMA,
        ],
        compiler_params=pltpu.CompilerParams(vmem_limit_bytes=24 * 2**20),
        name="update",
    )(weight, acts, rows, back)
    return grad_hidden, new_weights


def solution(mesh):
    return jax.shard_map(
        functools.partial(shards, mesh.shape["pipe"], mesh.shape["dp"]),
        mesh=mesh,
        in_specs=(
            P("pipe", None, None, "dp", None),
            P("pipe", None, None, None, "dp"),
            P("pipe", "dp", None),
            P("pipe", None, None, "dp"),
        ),
        out_specs=(P("pipe", None, None, None, "dp"), P("pipe", "dp", None)),
        check_vma=False,
    )
```

```python
import functools

import jax
import jax.numpy as jnp
from jax import lax
from jax.experimental import pallas as pl
from jax.experimental.pallas import tpu as pltpu
from jax.sharding import PartitionSpec as P

step_rate = 2.0
MESH = pl.DeviceIdType.MESH
LEFT, RIGHT, SIBLING = 0, 1, 2


def when(condition, action):
    if condition is True:
        action()
    else:
        pl.when(condition)(action)


def update_rows(factor, weight_ref, acts_ref, rows_ref, target_ref, first, count, target_first):
    high = 192 if count % 192 == 0 else count
    wide = 256 if weight_ref.shape[1] % 256 == 0 else 128
    for r in range(0, count, high):
        for c in range(0, weight_ref.shape[1], wide):
            columns = pl.ds(c, wide)
            total = jnp.dot(
                acts_ref[pl.ds(first + r, high), :], rows_ref[:, columns], preferred_element_type=jnp.float32
            )
            target_ref[pl.ds(target_first + r, high), columns] = (
                weight_ref[pl.ds(first + r, high), columns].astype(jnp.float32) - factor * total
            ).astype(jnp.bfloat16)


def gather_kernel(
    n_pipe, n_dp, scale_factor, chunk, early,
    counts_ref, grad_ref, hidden_ref, weights_ref,
    rows_ref, acts_ref, weight_out, out_ref,
    own_grad, staged, own_slot1, landed, acts_in, ret,
    send_sem, recv_sem, pair_send, pair_recv, ret_send, ret_recv, load_sem,
):
    p = lax.axis_index("pipe")
    k = lax.axis_index("dp")
    z = k // 2
    n = n_dp // 2
    mirror = (n_pipe - 1 - p, k)
    sibling = k + 1 - 2 * (k % 2)
    has_left = z > 0
    has_right = z < n - 1
    micro, row_total, width = grad_ref.shape[2], grad_ref.shape[3], grad_ref.shape[4]
    half = width // 2
    block_rows = micro * row_total
    group_rows = hidden_ref.shape[3]
    share = hidden_ref.shape[4]
    tokens = 2 * micro * group_rows

    load_grad = pltpu.make_async_copy(grad_ref.at[0], own_grad, load_sem.at[0])
    load_acts = pltpu.make_async_copy(hidden_ref.at[0, 0], acts_in.at[0], load_sem.at[1])
    load_weight = pltpu.make_async_copy(weights_ref.at[0], weight_out, load_sem.at[2])
    load_grad.start()

    barrier = pltpu.get_barrier_semaphore()
    pl.semaphore_signal(barrier, inc=1, device_id=mirror, device_id_type=MESH)
    pl.semaphore_signal(barrier, inc=1, device_id=(p, sibling), device_id_type=MESH)

    @pl.when(has_left)
    def _():
        pl.semaphore_signal(barrier, inc=1, device_id=(p, k - 2), device_id_type=MESH)

    @pl.when(has_right)
    def _():
        pl.semaphore_signal(barrier, inc=1, device_id=(p, k + 2), device_id_type=MESH)

    load_acts.start()
    load_weight.start()
    load_grad.wait()
    slot_index = lax.broadcasted_iota(jnp.int32, (row_total, width), 0)
    for r in (1, 0):
        for m in range(micro):
            live = slot_index < counts_ref[r, m]
            rows = jnp.where(live, own_grad[r, m].astype(jnp.float32), 0.0)
            for h in range(2):
                staged[r, pl.ds(h * block_rows + m * row_total, row_total), :] = rows[:, h * half:(h + 1) * half]
        packed = staged[r].astype(jnp.bfloat16)
        if r == 1:
            own_slot1[...] = packed
        else:
            landed[0, k] = packed

    pl.semaphore_wait(barrier, 2 + has_left.astype(jnp.int32) + has_right.astype(jnp.int32))

    cuts = (1, 2 if half % 256 == 0 else 1)

    def cut(s, part):
        return pl.ds(part * (half // cuts[s]), half // cuts[s])

    def hop(s, part, origin, way):
        target = {LEFT: k - 2, RIGHT: k + 2, SIBLING: sibling}[way]
        return pltpu.make_async_remote_copy(
            src_ref=landed.at[s, origin, :, cut(s, part)],
            dst_ref=landed.at[s, origin, :, cut(s, part)],
            send_sem=send_sem.at[s, part, origin, way],
            recv_sem=recv_sem.at[s, part, origin],
            device_id=(p, target),
            device_id_type=MESH,
        )

    def arrived(s, part, origin):
        hop(s, part, origin, SIBLING).wait_recv()

    mirror_rows = [
        pltpu.make_async_remote_copy(
            src_ref=own_slot1.at[:, cut(1, part)], dst_ref=landed.at[1, k, :, cut(1, part)],
            send_sem=pair_send.at[1 + part], recv_sem=recv_sem.at[1, part, k],
            device_id=mirror, device_id_type=MESH,
        )
        for part in range(cuts[1])
    ]
    mirror_acts = pltpu.make_async_remote_copy(
        src_ref=hidden_ref.at[0, 1], dst_ref=acts_in.at[1],
        send_sem=pair_send.at[0], recv_sem=pair_recv.at[0],
        device_id=mirror, device_id_type=MESH,
    )

    sent = []

    def send(s, part, origin, way, condition):
        sent.append((s, part, origin, way, condition))
        when(condition, lambda: hop(s, part, origin, way).start())

    def send_own(s, part):
        send(s, part, k, LEFT, has_left)
        send(s, part, k, RIGHT, has_right)
        send(s, part, k, SIBLING, True)

    def relay(s, j):
        from_left = z >= j
        from_right = z + j < n
        left_origin = jnp.maximum(k - 2 * j, 0)
        right_origin = jnp.minimum(k + 2 * j, n_dp - 1)
        for part in range(cuts[s]):
            pl.when(from_left)(functools.partial(arrived, s, part, left_origin))
            send(s, part, left_origin, RIGHT, jnp.logical_and(from_left, has_right))
            send(s, part, left_origin, SIBLING, from_left)
            pl.when(from_right)(functools.partial(arrived, s, part, right_origin))
            send(s, part, right_origin, LEFT, jnp.logical_and(from_right, has_left))
            send(s, part, right_origin, SIBLING, from_right)

    def drain():
        for s, part, origin, way, condition in sent:
            when(condition, functools.partial(lambda *a: hop(*a).wait_send(), s, part, origin, way))
        sent.clear()

    for copy in mirror_rows:
        copy.start()
    send_own(0, 0)
    for part in range(cuts[1]):
        arrived(1, part, k)
        send_own(1, part)
    mirror_acts.start()
    for j in range(1, n - 1):
        drain()
        relay(0, j)
        relay(1, j)

    at_token = lax.broadcasted_iota(jnp.int32, (tokens, tokens), 0)
    at_row = lax.broadcasted_iota(jnp.int32, (tokens, tokens), 1)
    slot, inside = at_token // (micro * group_rows), at_token % (micro * group_rows)
    of_micro, of_slot = inside // group_rows, inside % group_rows
    wanted = (
        slot * (micro * group_rows) + (of_slot // row_total) * block_rows
        + of_micro * row_total + of_slot % row_total
    )
    order = jnp.where(wanted == at_row, 1.0, 0.0).astype(jnp.bfloat16)

    load_acts.wait()
    mirror_acts.wait_recv()
    acts_ref[...] = lax.dot_general(
        acts_in[...].reshape(tokens, share), order,
        (((0,), (0,)), ((), ())), preferred_element_type=jnp.float32,
    ).astype(jnp.bfloat16)

    if n > 1:
        relay(1, n - 1)
        relay(0, n - 1)

    for s in range(2):
        for part in range(cuts[s]):
            arrived(s, part, sibling)
            for j in range(1, n):
                pl.when(z >= j)(functools.partial(arrived, s, part, jnp.maximum(sibling - 2 * j, 0)))
                pl.when(z + j < n)(
                    functools.partial(arrived, s, part, jnp.minimum(sibling + 2 * j, n_dp - 1))
                )
        for h in range(2):
            blocks = [
                landed[s, rank].astype(jnp.float32)[h * block_rows:(h + 1) * block_rows]
                for rank in range(n_dp)
            ]
            rows_ref[pl.ds(s * (tokens // 2), tokens // 2), pl.ds(h * half, half)] = jnp.concatenate(
                blocks, axis=0
            ).astype(jnp.bfloat16)
    load_weight.wait()

    def give_back(c):
        columns = pl.ds(c * chunk, chunk)
        return pltpu.make_async_remote_copy(
            src_ref=ret.at[:, :, columns], dst_ref=out_ref.at[0, 1, :, :, columns],
            send_sem=ret_send.at[c], recv_sem=ret_recv.at[c],
            device_id=mirror, device_id_type=MESH,
        )

    for c in range(share // chunk):
        columns = pl.ds(c * chunk, chunk)
        product = lax.dot_general(
            weight_out[columns, :], rows_ref[...],
            (((1,), (1,)), ((), ())), preferred_element_type=jnp.float32,
        )
        rounded = (product * scale_factor).astype(jnp.bfloat16)
        value = lax.dot_general(
            order, rounded, (((1,), (1,)), ((), ())), preferred_element_type=jnp.float32
        ).astype(jnp.bfloat16).reshape(2, micro, group_rows, chunk)
        ret[:, :, columns] = value[1]
        give_back(c).start()
        out_ref[0, 0, :, :, columns] = value[0]

    update_rows(step_rate * scale_factor, weight_out, acts_ref, rows_ref, weight_out, 0, early, 0)

    for copy in mirror_rows:
        copy.wait_send()
    mirror_acts.wait_send()
    drain()
    for c in range(share // chunk):
        give_back(c).wait()


def update_kernel(
    factor, early, step, weight_ref, acts_ref, rows_ref, back_ref, new_ref, out_ref, late, sems, out_sem
):
    put_back = pltpu.make_async_copy(back_ref, out_ref, out_sem)
    share = weight_ref.shape[0]

    def put(i):
        first = i * step
        source = weight_ref.at[pl.ds(first, step)] if first < early else late.at[pl.ds(first - early, step)]
        return pltpu.make_async_copy(source, new_ref.at[0, pl.ds(first, step)], sems.at[i])

    for i in range(early // step):
        put(i).start()
    put_back.start()
    for i in range(early // step, share // step):
        update_rows(factor, weight_ref, acts_ref, rows_ref, late, i * step, step, i * step - early)
        put(i).start()
    for i in range(share // step):
        put(i).wait()
    put_back.wait()


def shards(n_pipe, n_dp, grad_out, hidden, weights, counts):
    _, _, micro, row_total, width = grad_out.shape
    group_rows, share = hidden.shape[3], hidden.shape[4]
    block = 2 * micro * row_total
    half = width // 2
    tokens = 2 * micro * group_rows
    scale_factor = float(width) ** (-0.5)
    chunk = 384 if share % 384 == 0 else share
    early = 2 * (share // chunk) // 3 * chunk
    step = 192 if chunk % 192 == 0 else chunk
    vmem = pl.BlockSpec(memory_space=pltpu.VMEM)
    hbm = pl.BlockSpec(memory_space=pltpu.HBM)
    rows, acts, weight, back = pl.pallas_call(
        functools.partial(gather_kernel, n_pipe, n_dp, scale_factor, chunk, early),
        out_shape=(
            jax.ShapeDtypeStruct((tokens, width), jnp.bfloat16),
            jax.ShapeDtypeStruct((share, tokens), jnp.bfloat16),
            jax.ShapeDtypeStruct((share, width), jnp.bfloat16),
            jax.ShapeDtypeStruct(hidden.shape, jnp.bfloat16),
        ),
        in_specs=[pl.BlockSpec(memory_space=pltpu.SMEM), hbm, hbm, hbm],
        out_specs=(vmem, vmem, vmem, vmem),
        scratch_shapes=[
            pltpu.VMEM((2, micro, row_total, width), jnp.bfloat16),
            pltpu.VMEM((2, block, half), jnp.float32),
            pltpu.VMEM((block, half), jnp.bfloat16),
            pltpu.VMEM((2, n_dp, block, half), jnp.bfloat16),
            pltpu.VMEM((2, micro, group_rows, share), jnp.bfloat16),
            pltpu.VMEM((micro, group_rows, share), jnp.bfloat16),
            pltpu.SemaphoreType.DMA((2, 2, n_dp, 3)),
            pltpu.SemaphoreType.DMA((2, 2, n_dp)),
            pltpu.SemaphoreType.DMA((3,)),
            pltpu.SemaphoreType.DMA((1,)),
            pltpu.SemaphoreType.DMA((share // chunk,)),
            pltpu.SemaphoreType.DMA((share // chunk,)),
            pltpu.SemaphoreType.DMA((3,)),
        ],
        compiler_params=pltpu.CompilerParams(
            collective_id=0, has_side_effects=True, vmem_limit_bytes=42 * 2**20
        ),
        name="gather",
    )(*[pltpu.with_memory_space_constraint(x, pltpu.HBM) for x in (counts.reshape(2, micro), grad_out, hidden, weights)])
    new_weights, grad_hidden = pl.pallas_call(
        functools.partial(update_kernel, step_rate * scale_factor, early, step),
        out_shape=(
            jax.ShapeDtypeStruct(weights.shape, jnp.bfloat16),
            jax.ShapeDtypeStruct(hidden.shape, jnp.bfloat16),
        ),
        in_specs=[vmem, vmem, vmem, vmem],
        out_specs=(hbm, hbm),
        scratch_shapes=[
            pltpu.VMEM((share - early, width), jnp.bfloat16),
            pltpu.SemaphoreType.DMA((share // step,)),
            pltpu.SemaphoreType.DMA,
        ],
        compiler_params=pltpu.CompilerParams(vmem_limit_bytes=24 * 2**20),
        name="update",
    )(weight, acts, rows, back)
    return grad_hidden, new_weights


def solution(mesh):
    return jax.shard_map(
        functools.partial(shards, mesh.shape["pipe"], mesh.shape["dp"]),
        mesh=mesh,
        in_specs=(
            P("pipe", None, None, "dp", None),
            P("pipe", None, None, None, "dp"),
            P("pipe", "dp", None),
            P("pipe", None, None, "dp"),
        ),
        out_specs=(P("pipe", None, None, None, "dp"), P("pipe", "dp", None)),
        check_vma=False,
    )
```
